32 devices in a mesh: groups: 2 (over x), ckpt: 4 (over z), wide: 4 (over y, core).
Axes of the slice: x: 2, y: 2, z: 4, core: 2. Of those that a mesh axis runs over, the one named last changes fastest.
Arguments:
- query_grads: bfloat16 [4, 128, 32768], P('ckpt', 'groups', 'wide'), parts along dimension 1, may hold values from -6 to 6
- train_grads: bfloat16 [4, 512, 32768], P('ckpt', 'groups', 'wide'), parts along dimension 1, may hold values from -0.0059814453 to 0.0059814453
- step_rates: float32 [4], P('ckpt'), may hold values from 0.25 to 2
- layer_mask: int32 [4, 4, 4], P('wide'), may hold values from 0 to 1
- train_ids: int32 [256], replicated, may hold values from 0 to 255, each once
Outputs:
- influence: float32 [128, 256], P(('groups', 'ckpt', 'wide')), parts along dimension 0
The draws below stay inside these ranges and needn't reach their ends.
There are 2 independent parts, one for each index of `groups`. The reference program is written for one: setup_inputs(seed, part) draws one part's arguments, and reference() takes and returns one part's arrays. A program takes and returns all parts, laid end to end along the dimension named above; an argument that names none is the same for every part. Nothing has to cross between parts.
Inputs may be any that keep to these rules, and one draw needn't show every extreme that they name: `train_ids`: each stored row once.
All inputs are finite; a program needn't handle non-finite values.
Results may differ from the reference program's by a relative error of at most 0.0003.
Values sent between devices are 32-bit elements; how exact they have to be, the bound alone decides.
A program may use at most 64 MiB of HBM per device.

```python
import math
import jax
import jax.numpy as jnp
from jax import lax

P_SIZE = 8192
NT = 256
NQB = 4
NPAN = 4
CKPTS = 4
L = 4
NQ = 64


def draw_layer_mask(key, part):
    first_key, second_key = jax.random.split(key)
    density = jax.random.randint(first_key, (L, 1, 1), 1, 5)
    levels = jax.random.randint(second_key, (L, NQB, NPAN), 0, 4)
    return (levels < density).astype(jnp.int32)


def block_levels(own_key, dims, shards, smallest, high):
    def one(dim, parts):
        draws = jax.random.uniform(jax.random.fold_in(jax.random.fold_in(own_key, 6), dim), (parts,), jnp.float32, smallest / len(shards), high / len(shards))
        return jnp.repeat(jnp.exp(draws), dims[dim] // parts).reshape((-1,) + (1,) * (len(dims) - dim - 1))

    level = one(*shards[0])
    for cut in shards[1:]:
        level = level * one(*cut)
    return level


def scatter_about(stream_key, dims, spread, most, cuts=(), kind=jnp.bfloat16):
    gain = block_levels(stream_key, dims, cuts, -0.22, 0.18) if cuts else 1.0
    drawn = jax.random.normal(stream_key, dims, jnp.float32) * spread * gain
    return jnp.minimum(jnp.maximum(drawn, -most), most).astype(kind)


def setup_inputs(seed: int = 0, part: int = 0) -> dict:
    splits = jax.random.split(jax.random.key(seed), 6)
    part_keys = jax.random.split(jax.random.fold_in(splits[5], part), 6)
    return {
        "query_grads": scatter_about(part_keys[0], (CKPTS, NQ, L * P_SIZE), 1.0, 6.0, ((0, 4), (2, 4))),
        "train_grads": scatter_about(part_keys[1], (CKPTS, NT, L * P_SIZE), 0.001, 0.0059814453, ((0, 4), (2, 4))),
        "step_rates": jnp.clip(jnp.exp(math.log(2.0) - 2.0794415 * jax.random.uniform(splits[2], (CKPTS,), jnp.float32) ** block_levels(splits[2], (CKPTS,), ((0, 4),), -0.2, 0.2)), 0.25, 2.0),
        "layer_mask": draw_layer_mask(jax.random.fold_in(splits[5], 71), part),
        "train_ids": jax.random.permutation(splits[4], NT).astype(jnp.int32),
    }


def reference(query_grads, train_grads, step_rates, layer_mask, train_ids):
    chosen = jnp.take(train_grads, train_ids, axis=1)
    qblock = NQ // NQB
    panel = NT // NPAN

    def one_term(summed, flat_pos):
        ckpt_pos = flat_pos // L
        layer_pos = flat_pos % L
        zero_pos = jnp.int32(0)
        queries = lax.dynamic_slice(query_grads, (ckpt_pos, zero_pos, layer_pos * P_SIZE), (1, NQ, P_SIZE))[0]
        trained = lax.dynamic_slice(chosen, (ckpt_pos, zero_pos, layer_pos * P_SIZE), (1, NT, P_SIZE))[0]
        product = lax.dot_general(queries, trained, (((1,), (1,)), ((), ())), preferred_element_type=jnp.float32)
        weights = layer_mask[layer_pos].astype(jnp.float32)
        weights = jnp.repeat(jnp.repeat(weights, qblock, axis=0), panel, axis=1)
        return summed + step_rates[ckpt_pos] * weights * product, None

    summed, _ = lax.scan(one_term, jnp.zeros((NQ, NT), jnp.float32), jnp.arange(CKPTS * L, dtype=jnp.int32))
    return summed
```

```python
import functools

import jax
import jax.numpy as jnp
from jax import lax
from jax.experimental import pallas as pl
from jax.experimental.pallas import tpu as pltpu
from jax.sharding import PartitionSpec as P

NQB = 4
NPAN = 4
LANES = 128
KPARTS = 4
MESH = pl.DeviceIdType.MESH
DIMS = (((1,), (1,)), ((), ()))


def kernel(
    ckpts, wides,
    rate_hbm, mask_hbm, ids_hbm, q_hbm, t_hbm, out_ref,
    rate_ref, mask_ref, ids_ref, q_buf, t_buf, weights, sbuf, rbuf,
    s_sem, q_sem, t_sem, send_sem, recv_sem,
):
    n = ckpts * wides
    rows, depth = q_buf.shape
    cols = t_buf.shape[0]
    halves = cols // LANES
    own = rows // n
    step = depth // KPARTS
    group = lax.axis_index("groups")
    me = lax.axis_index("ckpt") * wides + lax.axis_index("wide")

    def q_copy(k):
        part = pl.ds(k * step, step)
        return pltpu.make_async_copy(q_hbm.at[0, :, part], q_buf.at[:, part], q_sem.at[k])

    def t_copy(h, k):
        part = pl.ds(k * step, step)
        some = pl.ds(h * LANES, LANES)
        return pltpu.make_async_copy(
            t_hbm.at[0, some, part], t_buf.at[some, part], t_sem.at[h, k]
        )

    small = [
        pltpu.make_async_copy(rate_hbm, rate_ref, s_sem.at[0]),
        pltpu.make_async_copy(mask_hbm, mask_ref, s_sem.at[1]),
        pltpu.make_async_copy(ids_hbm, ids_ref, s_sem.at[2]),
    ]
    for copy in small:
        copy.start()
    for h in range(halves):
        for k in range(KPARTS):
            if h == 0:
                q_copy(k).start()
            t_copy(h, k).start()

    def peer(r):
        where = lax.rem(me + r, n)
        return where, (group, where // wides, lax.rem(where, wides))

    barrier = pltpu.get_barrier_semaphore()
    for r in range(1, n):
        pl.semaphore_signal(barrier, inc=1, device_id=peer(r)[1], device_id_type=MESH)

    for copy in small:
        copy.wait()
    ids = ids_ref[...]
    hot = (lax.broadcasted_iota(jnp.int32, (cols, cols), 0) == ids).astype(jnp.bfloat16)
    panel = cols // NPAN
    in_panel = (
        lax.broadcasted_iota(jnp.int32, (16, cols), 1) // panel
        == lax.broadcasted_iota(jnp.int32, (16, cols), 0)
    ).astype(jnp.bfloat16)
    stored = lax.dot_general(in_panel, hot, DIMS, preferred_element_type=jnp.float32)
    qblock = rows // NQB
    rate = rate_ref[0]
    for b in range(NQB):
        row = sum(
            (rate * mask_ref[0, b, p].astype(jnp.float32)) * stored[p : p + 1, :]
            for p in range(NPAN)
        )
        weights[b * qblock : (b + 1) * qblock, :] = jnp.broadcast_to(row, (qblock, cols))

    pl.semaphore_wait(barrier, n - 1)

    for h in range(halves):
        some = slice(h * LANES, (h + 1) * LANES)
        product = None
        for k in range(KPARTS):
            if h == 0:
                q_copy(k).wait()
            t_copy(h, k).wait()
            part = slice(k * step, (k + 1) * step)
            term = lax.dot_general(
                q_buf[:, part], t_buf[some, part], DIMS, preferred_element_type=jnp.float32
            )
            product = term if product is None else product + term
        product = product * weights[:, some]
        for d in range(n):
            sbuf[h, d] = product[d * own : (d + 1) * own, :]
        for r in range(1, n):
            where, device = peer(r)
            pltpu.make_async_remote_copy(
                src_ref=sbuf.at[h, where],
                dst_ref=rbuf.at[h, r - 1],
                send_sem=send_sem.at[h],
                recv_sem=recv_sem.at[h],
                device_id=device,
                device_id_type=MESH,
            ).start()

    totals = []
    for h in range(halves):
        landed = rbuf.at[h]
        pltpu.make_async_copy(landed, landed, recv_sem.at[h]).wait()
        total = sbuf[h, me]
        for r in range(1, n):
            total = total + rbuf[h, r - 1]
        totals.append(total)

    for h in range(halves):
        some = slice(h * LANES, (h + 1) * LANES)
        wanted = jnp.broadcast_to(ids[:, some], (own, LANES))
        lane = wanted % LANES
        result = None
        for s in range(halves):
            got = jnp.take_along_axis(totals[s], lane, axis=1, mode="promise_in_bounds")
            result = got if result is None else jnp.where(wanted >= s * LANES, got, result)
        out_ref[:, some] = result

    for h in range(halves):
        gone = sbuf.at[h, pl.ds(0, n - 1)]
        pltpu.make_async_copy(gone, gone, send_sem.at[h]).wait()


def shards(ckpts, wides, query_grads, train_grads, step_rates, layer_mask, train_ids):
    n = ckpts * wides
    _, rows, depth = query_grads.shape
    cols = train_grads.shape[1]
    halves = cols // LANES
    own = rows // n
    return pl.pallas_call(
        functools.partial(kernel, ckpts, wides),
        out_shape=jax.ShapeDtypeStruct((own, cols), jnp.float32),
        in_specs=[
            pl.BlockSpec(memory_space=pltpu.HBM),
        ]
        * 5,
        out_specs=pl.BlockSpec(memory_space=pltpu.VMEM),
        scratch_shapes=[
            pltpu.SMEM(step_rates.shape, jnp.float32),
            pltpu.SMEM(layer_mask.shape, jnp.int32),
            pltpu.VMEM((1, cols), jnp.int32),
            pltpu.VMEM((rows, depth), jnp.bfloat16),
            pltpu.VMEM((cols, depth), jnp.bfloat16),
            pltpu.VMEM((rows, cols), jnp.float32),
            pltpu.VMEM((halves, n, own, LANES), jnp.float32),
            pltpu.VMEM((halves, n - 1, own, LANES), jnp.float32),
            pltpu.SemaphoreType.DMA((3,)),
            pltpu.SemaphoreType.DMA((KPARTS,)),
            pltpu.SemaphoreType.DMA((halves, KPARTS)),
            pltpu.SemaphoreType.DMA((halves,)),
            pltpu.SemaphoreType.DMA((halves,)),
        ],
        compiler_params=pltpu.CompilerParams(
            collective_id=0, has_side_effects=True, vmem_limit_bytes=64 * 1024 * 1024
        ),
        cost_estimate=pl.CostEstimate(
            flops=2 * rows * cols * depth,
            bytes_accessed=2 * (rows + cols) * depth,
            transcendentals=0,
        ),
    )(step_rates, layer_mask, train_ids.reshape(1, cols), query_grads, train_grads)


def solution(mesh):
    in_specs = (
        P("ckpt", "groups", "wide"),
        P("ckpt", "groups", "wide"),
        P("ckpt"),
        P("wide", None, None),
        P(),
    )
    out_specs = P(("groups", "ckpt", "wide"), None)
    body = functools.partial(shards, mesh.shape["ckpt"], mesh.shape["wide"])
    return jax.shard_map(body, mesh=mesh, in_specs=in_specs, out_specs=out_specs, check_vma=False)
```

```python
import functools
import math

import jax
import jax.numpy as jnp
from jax import lax
from jax.experimental import pallas as pl
from jax.experimental.pallas import tpu as pltpu
from jax.sharding import PartitionSpec as P

NQB = 4
NPAN = 4
LANES = 128
SPLITS = (8, 8)
STAGES = (("ckpt", "y", "core"),)
PRIORITY = (0, 0)
MESH = pl.DeviceIdType.MESH
DIMS = (((1,), (1,)), ((), ()))


def bounds(depth):
    total = sum(SPLITS)
    edges = [depth * sum(SPLITS[:k]) // total for k in range(len(SPLITS) + 1)]
    return list(zip(edges[:-1], edges[1:]))


def linear(names, at, sizes):
    place = 0
    for name in names:
        place = place * sizes[name] + at[name]
    return place


def unlinear(names, place, sizes):
    at = {}
    for name in reversed(names):
        at[name] = lax.rem(place, sizes[name])
        place = place // sizes[name]
    return at


def kernel(
    sizes,
    rate_hbm, mask_hbm, ids_hbm, q_hbm, t_hbm, out_ref,
    rate_ref, mask_ref, ids_ref, q_buf, t_buf, weights, *rest,
):
    stages = len(STAGES)
    send_bufs, recv_bufs = rest[:stages], rest[stages : 2 * stages]
    s_sem, q_sem, t_sem, send_sem, recv_sem = rest[2 * stages :]
    n = math.prod(sizes.values())
    rows, depth = q_buf.shape
    cols = t_buf.shape[0]
    own = rows // n
    group = lax.axis_index("groups")
    wide = lax.axis_index("wide")
    at = {"ckpt": lax.axis_index("ckpt"), "y": wide // 2, "core": lax.rem(wide, 2)}

    small = [
        pltpu.make_async_copy(rate_hbm, rate_ref, s_sem.at[0]),
        pltpu.make_async_copy(mask_hbm, mask_ref, s_sem.at[1]),
        pltpu.make_async_copy(ids_hbm, ids_ref, s_sem.at[2]),
    ]
    for copy in small:
        copy.start()
    big = []
    for k, (low, high) in enumerate(bounds(depth)):
        part = pl.ds(low, high - low)
        pair = (
            pltpu.make_async_copy(q_hbm.at[0, :, part], q_buf.at[:, part], q_sem.at[k]),
            pltpu.make_async_copy(t_hbm.at[0, :, part], t_buf.at[:, part], t_sem.at[k]),
        )
        for copy in pair:
            copy.start(priority=PRIORITY[k])
        big.append(pair)

    places, peers = [], []
    for names in STAGES:
        size = math.prod(sizes[name] for name in names)
        place = linear(names, at, sizes)
        places.append(place)
        some = []
        for r in range(1, size):
            there = lax.rem(place + r, size)
            to = {**at, **unlinear(names, there, sizes)}
            some.append((there, (group, to["ckpt"], to["y"] * 2 + to["core"])))
        peers.append(some)

    barrier = pltpu.get_barrier_semaphore()
    for some in peers:
        for _, device in some:
            pl.semaphore_signal(barrier, inc=1, device_id=device, device_id_type=MESH)

    for copy in small:
        copy.wait()
    ids = ids_ref[...]
    hot = (lax.broadcasted_iota(jnp.int32, (cols, cols), 0) == ids).astype(jnp.bfloat16)
    panel = cols // NPAN
    in_panel = (
        lax.broadcasted_iota(jnp.int32, (16, cols), 1) // panel
        == lax.broadcasted_iota(jnp.int32, (16, cols), 0)
    ).astype(jnp.bfloat16)
    stored = lax.dot_general(in_panel, hot, DIMS, preferred_element_type=jnp.float32)
    qblock = rows // NQB
    rate = rate_ref[0]
    for b in range(NQB):
        row = sum(
            (rate * mask_ref[0, b, p].astype(jnp.float32)) * stored[p : p + 1, :]
            for p in range(NPAN)
        )
        weights[b * qblock : (b + 1) * qblock, :] = jnp.broadcast_to(row, (qblock, cols))

    product = None
    for (low, high), pair in zip(bounds(depth), big):
        for copy in pair:
            copy.wait()
        term = lax.dot_general(
            t_buf[:, low:high], q_buf[:, low:high], DIMS, preferred_element_type=jnp.float32
        )
        product = term if product is None else product + term
    product = product.T * weights[...]

    for d in range(n):
        where = {"ckpt": d // (sizes["y"] * 2), "y": d // 2 % sizes["y"], "core": d % 2}
        order = [name for names in STAGES for name in names]
        send_bufs[0][linear(order, where, sizes)] = product[d * own : (d + 1) * own, :]

    pl.semaphore_wait(barrier, sum(len(some) for some in peers))

    left = n
    total = None
    for s, some in enumerate(peers):
        left = left // (len(some) + 1)
        for r, (there, device) in enumerate(some):
            pltpu.make_async_remote_copy(
                src_ref=send_bufs[s].at[pl.ds(there * left, left)],
                dst_ref=recv_bufs[s].at[pl.ds(r * left, left)],
                send_sem=send_sem.at[s],
                recv_sem=recv_sem.at[s],
                device_id=device,
                device_id_type=MESH,
            ).start()
        total = send_bufs[s][pl.ds(places[s] * left, left)]
        pltpu.make_async_copy(recv_bufs[s], recv_bufs[s], recv_sem.at[s]).wait()
        for r in range(len(some)):
            total = total + recv_bufs[s][r * left : (r + 1) * left]
        if s + 1 < stages:
            send_bufs[s + 1][...] = total
    total = total[0]

    halves = cols // LANES
    for h in range(halves):
        some = slice(h * LANES, (h + 1) * LANES)
        wanted = jnp.broadcast_to(ids[:, some], (own, LANES))
        lane = wanted % LANES
        result = None
        for s in range(halves):
            part = total[:, s * LANES : (s + 1) * LANES]
            got = jnp.take_along_axis(part, lane, axis=1, mode="promise_in_bounds")
            result = got if result is None else jnp.where(wanted >= s * LANES, got, result)
        out_ref[:, some] = result

    for s in range(stages):
        gone = recv_bufs[s]
        pltpu.make_async_copy(gone, gone, send_sem.at[s]).wait()


def shards(sizes, query_grads, train_grads, step_rates, layer_mask, train_ids):
    n = math.prod(sizes.values())
    _, rows, depth = query_grads.shape
    cols = train_grads.shape[1]
    own = rows // n
    send_shapes, recv_shapes, left = [], [], n
    for names in STAGES:
        size = math.prod(sizes[name] for name in names)
        send_shapes.append((left, own, cols))
        recv_shapes.append((left - left // size, own, cols))
        left = left // size
    in_hbm = [
        pltpu.with_memory_space_constraint(x, pltpu.HBM)
        for x in (layer_mask, train_ids.reshape(1, cols), query_grads, train_grads)
    ]
    return pl.pallas_call(
        functools.partial(kernel, sizes),
        out_shape=jax.ShapeDtypeStruct((own, cols), jnp.float32),
        in_specs=[pl.BlockSpec(memory_space=pltpu.HBM)] * 5,
        out_specs=pl.BlockSpec(memory_space=pltpu.VMEM),
        scratch_shapes=[
            pltpu.SMEM(step_rates.shape, jnp.float32),
            pltpu.SMEM(layer_mask.shape, jnp.int32),
            pltpu.VMEM((1, cols), jnp.int32),
            pltpu.VMEM((rows, depth), jnp.bfloat16),
            pltpu.VMEM((cols, depth), jnp.bfloat16),
            pltpu.VMEM((rows, cols), jnp.float32),
            *[pltpu.VMEM(shape, jnp.float32) for shape in send_shapes],
            *[pltpu.VMEM(shape, jnp.float32) for shape in recv_shapes],
            pltpu.SemaphoreType.DMA((3,)),
            pltpu.SemaphoreType.DMA((len(SPLITS),)),
            pltpu.SemaphoreType.DMA((len(SPLITS),)),
            pltpu.SemaphoreType.DMA((len(STAGES),)),
            pltpu.SemaphoreType.DMA((len(STAGES),)),
        ],
        compiler_params=pltpu.CompilerParams(
            collective_id=0, has_side_effects=True, vmem_limit_bytes=48 * 1024 * 1024
        ),
        cost_estimate=pl.CostEstimate(
            flops=2 * rows * cols * depth,
            bytes_accessed=2 * (rows + cols) * depth,
            transcendentals=0,
        ),
    )(step_rates, *in_hbm)


def solution(mesh):
    in_specs = (
        P("ckpt", "groups", "wide"),
        P("ckpt", "groups", "wide"),
        P("ckpt"),
        P("wide", None, None),
        P(),
    )
    out_specs = P(("groups", "ckpt", "wide"), None)
    sizes = {"ckpt": mesh.shape["ckpt"], "y": mesh.shape["wide"] // 2, "core": 2}
    body = functools.partial(shards, sizes)
    return jax.shard_map(body, mesh=mesh, in_specs=in_specs, out_specs=out_specs, check_vma=False)
```
